256 devices in a mesh: pipe: 4 (over z_hi), dp: 32 (over z_lo, x, y), tensor: 2 (over core).
Axes of the slice: x: 4, y: 4, z: 8 (z_hi: 4, z_lo: 2; z = z_hi * 2 + z_lo), core: 2. Of those that a mesh axis runs over, the one named last changes fastest.
Arguments:
- section_inputs: bfloat16 [4, 4096, 6144], P('pipe', 'dp', 'tensor'), may hold values from -256 to 256
- norm_gain: bfloat16 [4, 6144], P('pipe', 'tensor'), may hold values from 0.5 to 1.5
- down_proj: bfloat16 [4, 6144, 16], P('pipe', 'tensor'), may hold values from -0.078125 to 0.078125
- up_proj: bfloat16 [4, 16, 6144], P('pipe', None, 'tensor'), may hold values from -1.5 to 1.5
- top_grad: bfloat16 [4096, 6144], P('dp', 'tensor'), may hold values from -6 to 6
- lengths: int32 [32, 2], P('dp'), may hold values from 16 to 64, as said below
Outputs:
- section_grads: bfloat16 [4, 4096, 6144], P('pipe', 'dp', 'tensor')
- fac_input: float32 [4, 32, 2, 768, 768], P('pipe', 'dp', 'tensor')
- fac_output: float32 [4, 32, 2, 768, 768], P('pipe', 'dp', 'tensor')
The draws below stay inside these ranges and needn't reach their ends.
Inputs may be any that keep to these rules, and one draw needn't show every extreme that they name: `lengths`: each sequence has 64 positions; positions at or beyond its length are padding. Some sequence of every draw fills all 64.
All inputs are finite; a program needn't handle non-finite values.
Results may differ from the reference program's by a relative error of at most 0.0015.
The reference program's roundings to bfloat16 on the way count: a program that leaves them out, or rounds other values in their place, can miss the bound.
Values may be sent and summed in bfloat16 or wider, within the bound.
No kernel may reach another device: no remote copies, remote signals or barrier semaphores. Data moves between devices by JAX's collectives and lax.ppermute only.
A program may use at most 128 MiB of HBM per device.

```python
import math
import jax
import jax.numpy as jnp
from jax import lax

D = 6144
R = 16
LEN = 64
SECTIONS = 4
PAIRS = 32
TOKENS = 4096
ROWBLK = 768
COLBLK = 768
N_DP = 32
N_TENSOR = 2


def draw_section_inputs(key, part):
    key = jax.random.fold_in(key, 11)
    first, second, third = jax.random.split(key, 3)
    shape = (SECTIONS, TOKENS, D)
    ramp = jnp.arange(D, dtype=jnp.float32)[None, None, :] / D
    base = jax.random.truncated_normal(first, -4.0, 4.0, shape, jnp.float32)
    rows = jnp.exp(jax.random.uniform(second, (SECTIONS, TOKENS, 1), jnp.float32, math.log(0.3), math.log(3.0)))
    spread = math.log(10.0)
    cols = jnp.exp(spread * (0.5 * ramp + 0.5 * jax.random.uniform(third, (SECTIONS, 1, D), jnp.float32)))
    return (base * rows * cols).astype(jnp.bfloat16)


def draw_lengths(key, part):
    key = jax.random.fold_in(key, 23)
    values = jax.random.randint(key, (PAIRS, 2), LEN // 4, LEN + 1, dtype=jnp.int32)
    return values.at[0, 0].set(LEN)


def levels(rng, extent, cuts, smallest, high):
    level, own = 1.0, jax.random.fold_in(rng, 6)
    for dim, shards_of in cuts:
        steps = jnp.exp(jax.random.uniform(jax.random.fold_in(own, dim), (shards_of,), jnp.float32, smallest / len(cuts), high / len(cuts)))
        level = level * jnp.repeat(steps, extent[dim] // shards_of).reshape([-1 if axis == dim else 1 for axis in range(len(extent))])
    return level


def centred(key, extent, scale, bound, pieces=(), held_as=jnp.bfloat16):
    level = levels(key, extent, pieces, -0.22, 0.18) if pieces else 1.0
    drawn = jax.random.normal(key, extent, jnp.float32) * scale * level
    return jnp.minimum(jnp.maximum(drawn, -bound), bound).astype(held_as)


def setup_inputs(seed: int = 0) -> dict:
    key_of = jax.random.split(jax.random.key(seed), 7)
    return {
        "section_inputs": draw_section_inputs(jax.random.fold_in(key_of[6], 71), 0),
        "norm_gain": jnp.clip(1.0 + 0.1 * jax.random.normal(key_of[1], (SECTIONS, D), jnp.float32), 0.5, 1.5).astype(jnp.bfloat16),
        "down_proj": centred(key_of[2], (SECTIONS, D, R), D ** -0.5, 0.078125, ((0, 4), (1, 2))),
        "up_proj": centred(key_of[3], (SECTIONS, R, D), R ** -0.5, 1.5, ((0, 4), (2, 2))),
        "top_grad": centred(key_of[4], (TOKENS, D), 1.0, 6.0, ((0, 32), (1, 2))),
        "lengths": draw_lengths(jax.random.fold_in(key_of[6], 71), 0),
    }


adapter_scale = 0.5
epsilon_norm = 1e-05

def to_blocks(full):
    col_count = N_DP * N_TENSOR // 8
    tiles = full.reshape(8, ROWBLK, col_count, COLBLK).transpose(0, 2, 1, 3)
    return tiles.reshape(N_DP, N_TENSOR, ROWBLK, COLBLK)

def reference(section_inputs, norm_gain, down_proj, up_proj, top_grad, lengths):
    positions = jnp.arange(LEN, dtype=jnp.int32)
    valid = (positions[None, None, :] < lengths[:, :, None]).reshape(TOKENS, 1).astype(jnp.float32)
    grad = (top_grad.astype(jnp.float32) * valid).astype(jnp.bfloat16)
    grads_list = [None] * SECTIONS
    fin_list = [None] * SECTIONS
    fout_list = [None] * SECTIONS
    for section in range(SECTIONS - 1, -1, -1):
        x = section_inputs[section].astype(jnp.float32)
        gain = norm_gain[section].astype(jnp.float32)
        inverse = 1.0 / jnp.sqrt(lax.optimization_barrier(jnp.sum(x * x, axis=1, keepdims=True)) / D + epsilon_norm)
        normed = (x * inverse * gain * valid).astype(jnp.bfloat16)
        summed = jnp.dot(grad, up_proj[section].T, preferred_element_type=jnp.float32)
        low_grad = (adapter_scale * summed).astype(jnp.bfloat16)
        weighted = gain * jnp.dot(low_grad, down_proj[section].T, preferred_element_type=jnp.float32)
        inner = lax.optimization_barrier(jnp.sum(weighted * x, axis=1, keepdims=True))
        cube = inverse * inverse * inverse
        result = (grad.astype(jnp.float32) + inverse * weighted - x * cube * inner / D).astype(jnp.bfloat16)
        full_in = jnp.dot(normed.T, normed, preferred_element_type=jnp.float32) / TOKENS
        full_out = adapter_scale * adapter_scale * jnp.dot(grad.T, grad, preferred_element_type=jnp.float32) / TOKENS
        fin_list[section] = to_blocks(full_in)
        fout_list[section] = to_blocks(full_out)
        grads_list[section] = result
        grad = result
    return (jnp.stack(grads_list), jnp.stack(fin_list), jnp.stack(fout_list))
```

```python
import functools

import jax
import jax.numpy as jnp
from jax import lax
from jax.experimental import pallas as pl
from jax.experimental.pallas import tpu as pltpu
from jax.sharding import Mesh, PartitionSpec as P

D = 6144
HALF = D // 2
R = 16
LEN = 64
TOKENS = 4096
BLK = 768
NBLK = D // BLK
LOCAL = HALF // BLK
STAGES = 4
CHUNKS = 1
ROWS = LEN // CHUNKS

adapter_scale = 0.5
epsilon_norm = 1e-05

F32 = jnp.float32
BF16 = jnp.bfloat16
VMEM = pl.BlockSpec(memory_space=pltpu.VMEM)
PARAMS = pltpu.CompilerParams(vmem_limit_bytes=48 * 2**20)


def sds(shape, dtype):
    return jax.ShapeDtypeStruct(shape, dtype)


def ring(size, by):
    return [(i, (i + by) % size) for i in range(size)]


def prepare_kernel(
    info, x_own, top_own, w_own, received, x_out, top_out, normed_out, inverse_out, w_out
):
    core = info[0]
    length = info[1]
    valid = (lax.broadcasted_iota(jnp.int32, (LEN, 1), 0) < length).astype(F32)
    start = pl.multiple_of(core * LEN, LEN)
    squares = jnp.zeros((LEN, 1), F32)
    for i in range(LOCAL):
        cols = slice(i * BLK, (i + 1) * BLK)
        mine = core * LOCAL + i
        other = (1 - core) * LOCAL + i
        for place, x, top, w in (
            (mine, x_own[pl.ds(start, LEN), cols], top_own[pl.ds(start, LEN), cols], w_own[:, cols]),
            (other, received[0:LEN, cols], received[LEN : 2 * LEN, cols], received[2 * LEN :, cols]),
        ):
            x_out[place] = x
            top_out[place] = (top.astype(F32) * valid).astype(BF16)
            w_out[place] = w
            wide = x.astype(F32)
            squares += jnp.sum(wide * wide, axis=1, keepdims=True)
    inverse = 1.0 / jnp.sqrt(squares / D + epsilon_norm)
    inverse_out[...] = jnp.broadcast_to(inverse, (LEN, 128))
    for j in range(NBLK):
        gain = w_out[j, 2 * R : 2 * R + 1].astype(F32)
        normed_out[j] = (x_out[j].astype(F32) * inverse * gain * valid).astype(BF16)


def prepare(info, x, top, w, received):
    blocks = sds((NBLK, LEN, BLK), BF16)
    return pl.pallas_call(
        prepare_kernel,
        grid_spec=pltpu.PrefetchScalarGridSpec(
            num_scalar_prefetch=1, grid=(), in_specs=[VMEM] * 4, out_specs=[VMEM] * 5
        ),
        out_shape=[blocks, blocks, blocks, sds((LEN, 128), F32), sds((NBLK, 3 * R, BLK), BF16)],
        compiler_params=PARAMS,
        name="prepare",
    )(info, x, top, w, received)


def layer_kernel(use_received, info, received, current, x, inverse_in, w, current_out, result_out):
    total = jnp.zeros((ROWS, R), F32)
    fresh = info[3] if use_received else None
    for j in range(NBLK):
        grad = current[j]
        if use_received:
            grad = jnp.where(fresh == 1, received[j], grad)
        current_out[j] = grad
        total += lax.dot_general(
            grad, w[j, 0:R], (((1,), (1,)), ((), ())), preferred_element_type=F32
        )
    low = (adapter_scale * total).astype(BF16)
    inverse = inverse_in[:, 0:1]
    inner = jnp.zeros((ROWS, 1), F32)
    for j in range(NBLK):
        gain = w[j, 2 * R : 2 * R + 1].astype(F32)
        weighted = gain * jnp.dot(low, w[j, R : 2 * R], preferred_element_type=F32)
        inner += jnp.sum(weighted * x[j].astype(F32), axis=1, keepdims=True)
    cube = inverse * inverse * inverse
    scale = cube * inner / D
    for j in range(NBLK):
        gain = w[j, 2 * R : 2 * R + 1].astype(F32)
        weighted = gain * jnp.dot(low, w[j, R : 2 * R], preferred_element_type=F32)
        result_out[j] = (
            current_out[j].astype(F32) + inverse * weighted - x[j].astype(F32) * scale
        ).astype(BF16)


def layer(info, received, current, x, inverse, w):
    blocks = sds((NBLK, ROWS, BLK), BF16)
    use = received is not None
    if not use:
        received = current
    return pl.pallas_call(
        functools.partial(layer_kernel, use),
        grid_spec=pltpu.PrefetchScalarGridSpec(
            num_scalar_prefetch=1, grid=(), in_specs=[VMEM] * 5, out_specs=[VMEM] * 2
        ),
        out_shape=[blocks, blocks],
        compiler_params=PARAMS,
        name="layer",
    )(info, received, current, x, inverse, w)


def factor_kernel(scale, places, left, *rest):
    rights, out = rest[:8], rest[8]
    for i in range(8):
        rows = left[:, places[i]].reshape(8 * LEN, BLK)
        cols = rights[i][...].reshape(8 * LEN, BLK)
        part = lax.dot_general(
            rows, cols, (((0,), (0,)), ((), ())), preferred_element_type=F32
        )
        if i == 0:
            out[...] = part
        elif i < 7:
            out[...] += part
        else:
            out[...] = (out[...] + part) * scale


def factor(scale, places, left, rights):
    return pl.pallas_call(
        functools.partial(factor_kernel, scale),
        grid_spec=pltpu.PrefetchScalarGridSpec(
            num_scalar_prefetch=1, grid=(), in_specs=[VMEM] * 9, out_specs=VMEM
        ),
        out_shape=sds((BLK, BLK), F32),
        compiler_params=PARAMS,
        name="factor",
    )(places, left, *rights)


def gather_right(own):
    flip = functools.partial(lax.ppermute, axis_name="z", perm=ring(2, 1))
    from_next = functools.partial(lax.ppermute, axis_name="x", perm=ring(4, -1))
    from_prev = functools.partial(lax.ppermute, axis_name="x", perm=ring(4, 1))
    across = flip(own)
    nxt = from_next(own)
    prv = from_prev(own)
    far = from_next(nxt)
    across_prv = from_prev(across)
    across_nxt = flip(nxt)
    across_far = jnp.concatenate(
        [from_next(across_nxt[:3]), from_prev(across_prv[3:6]), flip(far[6:])], axis=0
    )
    return [own, across, nxt, prv, far, across_nxt, across_prv, across_far]


def blocks_of(tokens, scale, places):
    right = lax.all_to_all(tokens, ("y", "core"), split_axis=0, concat_axis=0, tiled=True)
    left = lax.all_to_all(tokens, ("z", "x"), split_axis=0, concat_axis=0, tiled=True)
    left = lax.all_gather(left, ("y", "core"), axis=0)
    rights = gather_right(right)
    return factor(scale, places, left, rights)


def per_device(section_inputs, norm_gain, down_proj, up_proj, top_grad, lengths):
    core = lax.axis_index("core")
    stage = lax.axis_index("pipe")
    here_z = lax.axis_index("z")
    here_x = lax.axis_index("x")
    swap = functools.partial(lax.ppermute, axis_name="core", perm=ring(2, 1))
    x = section_inputs[0]
    w = jnp.concatenate(
        [up_proj[0], down_proj[0].T, jnp.broadcast_to(norm_gain, (R, HALF))], axis=0
    )
    start = (1 - core) * LEN
    leaving = jnp.concatenate(
        [
            lax.dynamic_slice(x, (start, 0), (LEN, HALF)),
            lax.dynamic_slice(top_grad, (start, 0), (LEN, HALF)),
            w,
        ],
        axis=0,
    )
    received = swap(leaving)
    length = lax.dynamic_slice(lengths, (0, core), (1, 1))[0, 0]
    zero = jnp.zeros_like(length)
    x_blocks, current, normed, inverse, w_blocks = prepare(
        jnp.stack([core, length]), x, top_grad, w, received
    )

    places = jnp.stack(
        [
            z * 4 + (here_x + dx) % 4
            for z, dx in (
                (here_z, 0),
                (1 - here_z, 0),
                (here_z, 1),
                (here_z, 3),
                (here_z, 2),
                (1 - here_z, 1),
                (1 - here_z, 3),
                (1 - here_z, 2),
            )
        ]
    ).astype(jnp.int32)

    fac_in = blocks_of(normed, 1.0 / TOKENS, places)

    incoming = None
    for step in range(STAGES):
        fresh = (stage == STAGES - 1 - step).astype(jnp.int32)
        info = jnp.stack([zero, zero, zero, fresh])
        current, result = layer(info, incoming, current, x_blocks, inverse, w_blocks)
        if step + 1 < STAGES:
            incoming = lax.ppermute(result, "pipe", [(STAGES - 1 - step, STAGES - 2 - step)])
    fac_out = blocks_of(current, adapter_scale * adapter_scale / TOKENS, places)

    rows = result.reshape(2, LOCAL, LEN, BLK)
    mine = lax.dynamic_index_in_dim(rows, core, 0, keepdims=False)
    other = swap(lax.dynamic_index_in_dim(rows, 1 - core, 0, keepdims=False))
    pair = jnp.stack([mine, other])
    pair = jnp.where(core == 0, pair, pair[::-1])
    grads = pair.transpose(0, 2, 1, 3).reshape(1, 2 * LEN, HALF)
    return (grads, fac_in[None, None, None], fac_out[None, None, None])


def solution(mesh):
    fine = Mesh(mesh.devices.reshape(4, 2, 4, 4, 2), ("pipe", "z", "x", "y", "core"))
    dp = ("z", "x", "y")
    placed = (
        P("pipe", dp, "core"),
        P("pipe", "core"),
        P("pipe", "core", None),
        P("pipe", None, "core"),
        P(dp, "core"),
        P(dp, None),
    )
    return jax.shard_map(
        per_device,
        mesh=fine,
        in_specs=placed,
        out_specs=(
            P("pipe", dp, "core"),
            P("pipe", dp, "core", None, None),
            P("pipe", dp, "core", None, None),
        ),
        check_vma=False,
    )
```

```python
import functools

import jax
import jax.numpy as jnp
from jax import lax
from jax.experimental import pallas as pl
from jax.experimental.pallas import tpu as pltpu
from jax.sharding import Mesh, PartitionSpec as P

D = 6144
HALF = D // 2
R = 16
LEN = 64
TOKENS = 4096
BLK = 768
NBLK = D // BLK
LOCAL = HALF // BLK
STAGES = 4
CHUNKS = 2
ROWS = LEN // CHUNKS

adapter_scale = 0.5
epsilon_norm = 1e-05

F32 = jnp.float32
BF16 = jnp.bfloat16
VMEM = pl.BlockSpec(memory_space=pltpu.VMEM)
PARAMS = pltpu.CompilerParams(vmem_limit_bytes=12 * 2**20)


def sds(shape, dtype):
    return jax.ShapeDtypeStruct(shape, dtype)


def ring(size, by):
    return [(i, (i + by) % size) for i in range(size)]


def prepare_kernel(
    info, x_own, top_own, w_own, received, x_out, top_out, normed_out, w_out
):
    core = info[0]
    length = info[1]
    valid = (lax.broadcasted_iota(jnp.int32, (LEN, 1), 0) < length).astype(F32)
    start = pl.multiple_of(core * LEN, LEN)
    squares = jnp.zeros((LEN, 1), F32)
    for i in range(LOCAL):
        cols = slice(i * BLK, (i + 1) * BLK)
        mine = core * LOCAL + i
        other = (1 - core) * LOCAL + i
        for place, x, top, w in (
            (mine, x_own[pl.ds(start, LEN), cols], top_own[pl.ds(start, LEN), cols], w_own[:, cols]),
            (other, received[0:LEN, cols], received[LEN : 2 * LEN, cols], received[2 * LEN :, cols]),
        ):
            x_out[place] = x
            top_out[place] = (top.astype(F32) * valid).astype(BF16)
            w_out[place] = w
            wide = x.astype(F32)
            squares += jnp.sum(wide * wide, axis=1, keepdims=True)
    inverse = 1.0 / jnp.sqrt(squares / D + epsilon_norm)
    for j in range(NBLK):
        gain = w_out[j, 2 * R : 2 * R + 1].astype(F32)
        normed_out[j] = (x_out[j].astype(F32) * inverse * gain * valid).astype(BF16)


def prepare(info, x, top, w, received):
    blocks = sds((NBLK, LEN, BLK), BF16)
    return pl.pallas_call(
        prepare_kernel,
        grid_spec=pltpu.PrefetchScalarGridSpec(
            num_scalar_prefetch=1, grid=(), in_specs=[VMEM] * 4, out_specs=[VMEM] * 4
        ),
        out_shape=[blocks, blocks, blocks, sds((NBLK, 3 * R, BLK), BF16)],
        compiler_params=PARAMS,
        name="prepare",
    )(info, x, top, w, received)


def layer_kernel(slot, info, top, x, w, *refs):
    received = refs[0] if slot else None
    current, result, leaving = refs[-3:]
    stage = info[2]
    chunk = slot - (STAGES - 1) + stage

    @pl.when(jnp.logical_and(chunk >= 0, chunk < CHUNKS))
    def _():
        rows = pl.ds(pl.multiple_of(chunk * ROWS, ROWS), ROWS)
        total = jnp.zeros((ROWS, R), F32)
        squares = jnp.zeros((ROWS, 1), F32)
        for j in range(NBLK):
            grad = top[j, rows]
            if slot:
                grad = jnp.where(stage == STAGES - 1, grad, received[j])
            current[j, rows] = grad
            total += lax.dot_general(
                grad, w[j, 0:R], (((1,), (1,)), ((), ())), preferred_element_type=F32
            )
            wide = x[j, rows].astype(F32)
            squares += jnp.sum(wide * wide, axis=1, keepdims=True)
        low = (adapter_scale * total).astype(BF16)
        inverse = 1.0 / jnp.sqrt(squares / D + epsilon_norm)
        inner = jnp.zeros((ROWS, 1), F32)

        def weighted(j):
            gain = w[j, 2 * R : 2 * R + 1].astype(F32)
            return gain * jnp.dot(low, w[j, R : 2 * R], preferred_element_type=F32)

        for j in range(NBLK):
            inner += jnp.sum(weighted(j) * x[j, rows].astype(F32), axis=1, keepdims=True)
        cube = inverse * inverse * inverse
        scale = cube * inner / D
        for j in range(NBLK):
            value = (
                current[j, rows].astype(F32)
                + inverse * weighted(j)
                - x[j, rows].astype(F32) * scale
            ).astype(BF16)
            result[j, rows] = value
            leaving[j] = value


def layer(slot, info, top, x, w, received, before):
    blocks = sds((NBLK, LEN, BLK), BF16)
    args = [top, x, w] + ([received] if slot else []) + list(before)
    at = len(args) - 1
    return pl.pallas_call(
        functools.partial(layer_kernel, slot),
        grid_spec=pltpu.PrefetchScalarGridSpec(
            num_scalar_prefetch=1, grid=(), in_specs=[VMEM] * len(args), out_specs=[VMEM] * 3
        ),
        out_shape=[blocks, blocks, sds((NBLK, ROWS, BLK), BF16)],
        input_output_aliases={at: 0, at + 1: 1} if before else {},
        compiler_params=PARAMS,
        name="layer",
    )(info, *args)


def move_down(slot, leaving):
    pairs = [(s, s - 1) for s in range(1, STAGES) if 0 <= slot - (STAGES - 1) + s < CHUNKS]
    return lax.ppermute(leaving, "pipe", pairs)


def factor_kernel(counts, places, left, *refs):
    rights, out = refs[:-1], refs[-1]
    for n, count in enumerate(counts):
        rows = left[:, places[n]].reshape(8 * LEN, BLK)
        chunk, rights = rights[:count], rights[count:]
        cols = jnp.concatenate([piece[...].reshape(-1, BLK) for piece in chunk], axis=0)
        part = lax.dot_general(
            rows, cols, (((0,), (0,)), ((), ())), preferred_element_type=F32
        )
        out[...] = out[...] + part if n else part


def factor(places, left, rights):
    pieces = [piece for chunk in rights for piece in chunk]
    counts = tuple(len(chunk) for chunk in rights)
    return pl.pallas_call(
        functools.partial(factor_kernel, counts),
        grid_spec=pltpu.PrefetchScalarGridSpec(
            num_scalar_prefetch=1, grid=(), in_specs=[VMEM] * (1 + len(pieces)), out_specs=VMEM
        ),
        out_shape=sds((BLK, BLK), F32),
        compiler_params=PARAMS,
        cost_estimate=pl.CostEstimate(
            flops=16 * LEN * BLK * BLK * len(counts),
            bytes_accessed=32 * LEN * BLK * len(counts) + 4 * BLK * BLK,
            transcendentals=0,
        ),
        name="factor",
    )(places, left, *pieces)


def finish_kernel(scale, begun, left, *refs):
    pieces, out = refs[:-1], refs[-1]
    cols = jnp.concatenate([piece[...].reshape(-1, BLK) for piece in pieces], axis=0)
    part = lax.dot_general(
        left[...].reshape(8 * LEN, BLK),
        cols,
        (((0,), (0,)), ((), ())),
        preferred_element_type=F32,
    )
    out[...] = (begun[...] + part) * scale


def finish(scale, begun, left, pieces):
    return pl.pallas_call(
        functools.partial(finish_kernel, scale),
        in_specs=[VMEM] * (2 + len(pieces)),
        out_specs=VMEM,
        out_shape=sds((BLK, BLK), F32),
        compiler_params=PARAMS,
        name="finish",
    )(begun, left, *pieces)


def fence(*groups):
    leaves, tree = jax.tree.flatten(groups)
    return jax.tree.unflatten(tree, lax.optimization_barrier(tuple(leaves)))


def split_kernel(info, tokens, to_core, to_z):
    core, z = info[0], info[4]
    for q in range(4):
        to_core[q] = tokens[2 * q + 1 - core]
        to_z[q] = tokens[4 * (1 - z) + q]


def pack_kernel(info, tokens, from_core, from_z, *outs):
    core, z, x, y = info[0], info[4], info[5], info[6]
    for k in range(4):
        place = lax.rem(y + k, 4)
        outs[k][core] = tokens[2 * place + core]
        outs[k][1 - core] = from_core[place]
        place = lax.rem(x + k, 4)
        outs[4 + k][z] = tokens[4 * z + place]
        outs[4 + k][1 - z] = from_z[place]


def assemble_kernel(info, *refs):
    along_y, along_x, (right, left) = refs[:4], refs[4:8], refs[8:]
    x, y = info[5], info[6]
    for k in range(4):
        place_y = lax.rem(y + 4 - k, 4)
        place_x = lax.rem(x + 4 - k, 4)
        for h in range(2):
            right[2 * place_y + h] = along_y[k][h]
            left[4 * h + place_x] = along_x[k][h]


def local(kernel, name, outs, *args):
    return pl.pallas_call(
        kernel,
        grid_spec=pltpu.PrefetchScalarGridSpec(
            num_scalar_prefetch=1,
            grid=(),
            in_specs=[VMEM] * (len(args) - 1),
            out_specs=[VMEM] * len(outs),
        ),
        out_shape=[sds((n, LEN, BLK), BF16) for n in outs],
        compiler_params=PARAMS,
        name=name,
    )(*args)


def shifts(arrays, axis):
    return [lax.ppermute(a, axis, ring(4, k)) for k, a in enumerate(arrays, 1)]


def first_move(info, tokens):
    to_core, to_z = local(split_kernel, "split", [4, 4], info, tokens)
    return [swap(to_core), flip(to_z)]


def second_move(info, tokens, from_core, from_z):
    packs = local(pack_kernel, "pack", [2] * 8, info, tokens, from_core, from_z)
    return [packs[0], *shifts(packs[1:4], "y"), packs[4], *shifts(packs[5:], "x")]


def assemble(info, *pieces):
    return local(assemble_kernel, "assemble", [8, 8], info, *pieces)


def swap(a):
    return lax.ppermute(a, "core", ring(2, 1))


def gather_left(left):
    return lax.all_gather(left, ("y", "core"), axis=0)


def from_next(a):
    return lax.ppermute(a, "x", ring(4, -1))


def from_prev(a):
    return lax.ppermute(a, "x", ring(4, 1))


def flip(a):
    return lax.ppermute(a, "z", ring(2, 1))


def gather_first(own):
    return [flip(own), from_next(own), from_prev(own)]


def gather_second(across, nxt, prv):
    return [from_next(nxt), flip(nxt), from_prev(across)]


def gather_third(far, across_nxt, across_prv):
    return [from_next(across_nxt[:3]), from_prev(across_prv[3:6]), flip(far[6:])]


def per_device(section_inputs, norm_gain, down_proj, up_proj, top_grad, lengths):
    core = lax.axis_index("core")
    stage = lax.axis_index("pipe")
    here_z = lax.axis_index("z")
    here_x = lax.axis_index("x")
    x = section_inputs[0]
    down_t = down_proj[0].T
    w = jnp.concatenate(
        [up_proj[0], down_t, jnp.broadcast_to(norm_gain, (R, HALF))], axis=0
    )
    start = (1 - core) * LEN
    leaving = jnp.concatenate(
        [
            lax.dynamic_slice(x, (start, 0), (LEN, HALF)),
            lax.dynamic_slice(top_grad, (start, 0), (LEN, HALF)),
            w,
        ],
        axis=0,
    )
    received = swap(leaving)
    length = lax.dynamic_slice(lengths, (0, core), (1, 1))[0, 0]
    info = jnp.stack(
        [core, length, stage, jnp.zeros_like(stage), here_z, here_x, lax.axis_index("y")]
    ).astype(jnp.int32)
    x_blocks, top, normed, w_blocks = prepare(info, x, top_grad, w, received)
    places = jnp.stack(
        [
            z * 4 + (here_x + dx) % 4
            for z, dx in (
                (here_z, 0),
                (1 - here_z, 0),
                (here_z, 1),
                (here_z, 3),
                (here_z, 2),
                (1 - here_z, 1),
                (1 - here_z, 3),
                (1 - here_z, 2),
            )
        ]
    ).astype(jnp.int32)

    def step(slot, received, before):
        return layer(slot, info, top, x_blocks, w_blocks, received, before)

    *state, leaving = step(0, None, ())
    above = move_down(0, leaving)
    moved = first_move(info, normed)
    above, moved, state, normed = fence(above, moved, state, normed)

    *state, leaving = step(1, above, state)
    above = move_down(1, leaving)
    moved_again = second_move(info, normed, *moved)
    above, moved_again, state, normed = fence(above, moved_again, state, normed)

    *state, leaving = step(2, above, state)
    above = move_down(2, leaving)
    own_in, left_in = assemble(info, *moved_again)
    left_in = gather_left(left_in)
    nxt, prv = from_next(own_in), from_prev(own_in)
    above, nxt, prv, own_in, state = fence(above, nxt, prv, own_in, state)

    *state, leaving = step(3, above, state)
    above = move_down(3, leaving)
    far = [from_next(nxt[:4]), from_prev(prv[4:])]
    across = flip(own_in)
    above, far, across, state, own_in = fence(above, far, across, state, own_in)
    current, result, _ = step(4, above, state)

    moved = first_move(info, current)
    across_nxt, across_prv = from_next(across), from_prev(across)
    moved, across_nxt, across_prv, current, result = fence(
        moved, across_nxt, across_prv, current, result
    )

    moved_again = second_move(info, current, *moved)
    moved_again, result = fence(moved_again, result)

    own_out, left_out = assemble(info, *moved_again)
    left_out = gather_left(left_out)
    first_out = gather_first(own_out)
    third_in = [from_next(across_nxt[:3]), from_prev(across_prv[3:6]), flip(far[1][2:])]
    rights_in = [[own_in], [across], [nxt], [prv], far, [across_nxt], [across_prv]]
    begun_in = factor(places, left_in, rights_in)
    halves = result.reshape(2, LOCAL, LEN, BLK)
    mine = lax.dynamic_index_in_dim(halves, core, 0, keepdims=False)
    other = swap(lax.dynamic_index_in_dim(halves, 1 - core, 0, keepdims=False))
    pair = jnp.where(core == 0, jnp.stack([mine, other]), jnp.stack([other, mine]))
    grads = pair.transpose(0, 2, 1, 3).reshape(1, 2 * LEN, HALF)
    last_in = lax.dynamic_index_in_dim(left_in, places[7], 1, keepdims=False)
    first_out, third_in, begun_in, last_in, grads = fence(
        first_out, third_in, begun_in, last_in, grads
    )
    second_out = gather_second(*first_out)
    fac_in = finish(1.0 / TOKENS, begun_in, last_in, third_in)
    second_out, fac_in = fence(second_out, fac_in)
    third_out = gather_third(*second_out)
    begun = factor(places, left_out, [[a] for a in (own_out, *first_out, *second_out)])
    last_out = lax.dynamic_index_in_dim(left_out, places[7], 1, keepdims=False)
    third_out, begun, last_out = fence(third_out, begun, last_out)
    fac_out = finish(adapter_scale * adapter_scale / TOKENS, begun, last_out, third_out)
    return (grads, fac_in[None, None, None], fac_out[None, None, None])


def solution(mesh):
    fine = Mesh(mesh.devices.reshape(4, 2, 4, 4, 2), ("pipe", "z", "x", "y", "core"))
    dp = ("z", "x", "y")
    placed = (
        P("pipe", dp, "core"),
        P("pipe", "core"),
        P("pipe", "core", None),
        P("pipe", None, "core"),
        P(dp, "core"),
        P(dp, None),
    )
    return jax.shard_map(
        per_device,
        mesh=fine,
        in_specs=placed,
        out_specs=(
            P("pipe", dp, "core"),
            P("pipe", dp, "core", None, None),
            P("pipe", dp, "core", None, None),
        ),
        check_vma=False,
    )
```

```python
import functools

import jax
import jax.numpy as jnp
from jax import lax
from jax.experimental import pallas as pl
from jax.experimental.pallas import tpu as pltpu
from jax.sharding import Mesh, PartitionSpec as P

D = 6144
HALF = D // 2
R = 16
LEN = 64
TOKENS = 4096
BLK = 768
NBLK = D // BLK
LOCAL = HALF // BLK
STAGES = 4
CHUNKS = 2
ROWS = LEN // CHUNKS

adapter_scale = 0.5
epsilon_norm = 1e-05

F32 = jnp.float32
BF16 = jnp.bfloat16
VMEM = pl.BlockSpec(memory_space=pltpu.VMEM)
PARAMS = pltpu.CompilerParams(vmem_limit_bytes=12 * 2**20)


def sds(shape, dtype):
    return jax.ShapeDtypeStruct(shape, dtype)


def ring(size, by):
    return [(i, (i + by) % size) for i in range(size)]


def prepare_kernel(info, x, top, *refs):
    halves = (refs[:3], refs[5:8])
    others = refs[3:5]
    x_out, top_out, normed_out, w_out = refs[8:]
    core, length = info[0], info[1]
    valid = (lax.broadcasted_iota(jnp.int32, (LEN, 1), 0) < length).astype(F32)
    rows = pl.ds(pl.multiple_of(core * LEN, LEN), LEN)
    squares = jnp.zeros((LEN, 1), F32)
    for i in range(LOCAL):
        cols = slice(i * BLK, (i + 1) * BLK)
        for side, x_part, top_part, (up, down, gain) in (
            (core, x[rows, cols], top[rows, cols], halves[0]),
            (1 - core, others[0][:, cols], others[1][:, cols], halves[1]),
        ):
            place = side * LOCAL + i
            x_out[place] = x_part
            top_out[place] = (top_part.astype(F32) * valid).astype(BF16)
            w_out[place, 0:R] = up[:, cols]
            w_out[place, R : 2 * R] = down[:, cols]
            w_out[place, 2 * R :] = jnp.broadcast_to(gain[:, cols], (R, BLK))
            wide = x_part.astype(F32)
            squares += jnp.sum(wide * wide, axis=1, keepdims=True)
    inverse = 1.0 / jnp.sqrt(squares / D + epsilon_norm)
    for j in range(NBLK):
        gain = w_out[j, 2 * R : 2 * R + 1].astype(F32)
        normed_out[j] = (x_out[j].astype(F32) * inverse * gain * valid).astype(BF16)


def prepare(info, *args):
    blocks = sds((NBLK, LEN, BLK), BF16)
    return pl.pallas_call(
        prepare_kernel,
        grid_spec=pltpu.PrefetchScalarGridSpec(
            num_scalar_prefetch=1, grid=(), in_specs=[VMEM] * 10, out_specs=[VMEM] * 4
        ),
        out_shape=[blocks, blocks, blocks, sds((NBLK, 3 * R, BLK), BF16)],
        compiler_params=PARAMS,
        name="prepare",
    )(info, *args)


def layer_kernel(slot, info, top, x, w, *refs):
    received = refs[0] if slot else None
    current, result, leaving = refs[-3:]
    stage = info[2]
    chunk = slot - (STAGES - 1) + stage

    @pl.when(jnp.logical_and(chunk >= 0, chunk < CHUNKS))
    def _():
        rows = pl.ds(pl.multiple_of(chunk * ROWS, ROWS), ROWS)
        total = jnp.zeros((ROWS, R), F32)
        squares = jnp.zeros((ROWS, 1), F32)
        for j in range(NBLK):
            grad = top[j, rows]
            if slot:
                grad = jnp.where(stage == STAGES - 1, grad, received[j])
            current[j, rows] = grad
            total += lax.dot_general(
                grad, w[j, 0:R], (((1,), (1,)), ((), ())), preferred_element_type=F32
            )
            wide = x[j, rows].astype(F32)
            squares += jnp.sum(wide * wide, axis=1, keepdims=True)
        low = (adapter_scale * total).astype(BF16)
        inverse = 1.0 / jnp.sqrt(squares / D + epsilon_norm)
        inner = jnp.zeros((ROWS, 1), F32)

        def weighted(j):
            gain = w[j, 2 * R : 2 * R + 1].astype(F32)
            return gain * jnp.dot(low, w[j, R : 2 * R], preferred_element_type=F32)

        for j in range(NBLK):
            inner += jnp.sum(weighted(j) * x[j, rows].astype(F32), axis=1, keepdims=True)
        cube = inverse * inverse * inverse
        scale = cube * inner / D
        for j in range(NBLK):
            value = (
                current[j, rows].astype(F32)
                + inverse * weighted(j)
                - x[j, rows].astype(F32) * scale
            ).astype(BF16)
            result[j, rows] = value
            leaving[j] = value


def layer(slot, info, top, x, w, received, before):
    blocks = sds((NBLK, LEN, BLK), BF16)
    args = [top, x, w] + ([received] if slot else []) + list(before)
    at = len(args) - 1
    return pl.pallas_call(
        functools.partial(layer_kernel, slot),
        grid_spec=pltpu.PrefetchScalarGridSpec(
            num_scalar_prefetch=1, grid=(), in_specs=[VMEM] * len(args), out_specs=[VMEM] * 3
        ),
        out_shape=[blocks, blocks, sds((NBLK, ROWS, BLK), BF16)],
        input_output_aliases={at: 0, at + 1: 1} if before else {},
        compiler_params=PARAMS,
        name="layer",
    )(info, *args)


def move_down(slot, leaving):
    pairs = [(s, s - 1) for s in range(1, STAGES) if 0 <= slot - (STAGES - 1) + s < CHUNKS]
    return lax.ppermute(leaving, "pipe", pairs)


def factor_kernel(scale, counts, first, places, left, *refs):
    pieces, refs = refs[: sum(counts)], refs[sum(counts) :]
    before = refs[0] if first else None
    out, rows, cols, sems = refs[-4:]
    copies = []
    for n, count in enumerate(counts):
        chunk, pieces = pieces[:count], pieces[count:]
        pairs = [(left.at[:, places[first + n]], rows.at[n])]
        at = 0
        for piece in chunk:
            size = piece.shape[0]
            pairs.append((piece, cols.at[n, at : at + size]))
            at += size
        copies.append(
            [
                pltpu.make_async_copy(source, target, sems.at[n, i])
                for i, (source, target) in enumerate(pairs)
            ]
        )
        for copy in copies[n]:
            copy.start()
    for n in range(len(counts)):
        for copy in copies[n]:
            copy.wait()
        part = lax.dot_general(
            rows[n].reshape(8 * LEN, BLK),
            cols[n].reshape(8 * LEN, BLK),
            (((0,), (0,)), ((), ())),
            preferred_element_type=F32,
        )
        if n or first:
            part = (out if n else before)[...] + part
        out[...] = part * scale if scale != 1.0 and n == len(counts) - 1 else part


def factor(scale, places, left, rights, before=None, first=0):
    pieces = [piece for chunk in rights for piece in chunk]
    counts = tuple(len(chunk) for chunk in rights)
    begun = [] if before is None else [before]
    chunks = pltpu.VMEM((len(counts), 8, LEN, BLK), BF16)
    return pl.pallas_call(
        functools.partial(factor_kernel, scale, counts, first),
        grid_spec=pltpu.PrefetchScalarGridSpec(
            num_scalar_prefetch=1,
            grid=(),
            in_specs=[pl.BlockSpec(memory_space=pl.ANY)] * (1 + len(pieces))
            + [VMEM] * len(begun),
            out_specs=VMEM,
            scratch_shapes=[
                chunks,
                chunks,
                pltpu.SemaphoreType.DMA((len(counts), 1 + max(counts))),
            ],
        ),
        out_shape=sds((BLK, BLK), F32),
        compiler_params=pltpu.CompilerParams(vmem_limit_bytes=56 * 2**20),
        cost_estimate=pl.CostEstimate(
            flops=16 * LEN * BLK * BLK * len(counts),
            bytes_accessed=32 * LEN * BLK * len(counts) + 4 * BLK * BLK,
            transcendentals=0,
        ),
        name="factor",
    )(places, left, *pieces, *begun)


def finish_kernel(scale, begun, left, *refs):
    pieces, out = refs[:-1], refs[-1]
    cols = jnp.concatenate([piece[...].reshape(-1, BLK) for piece in pieces], axis=0)
    part = lax.dot_general(
        left[...].reshape(8 * LEN, BLK),
        cols,
        (((0,), (0,)), ((), ())),
        preferred_element_type=F32,
    )
    out[...] = (begun[...] + part) * scale


def finish(scale, begun, left, pieces):
    return pl.pallas_call(
        functools.partial(finish_kernel, scale),
        in_specs=[VMEM] * (2 + len(pieces)),
        out_specs=VMEM,
        out_shape=sds((BLK, BLK), F32),
        compiler_params=PARAMS,
        name="finish",
    )(begun, left, *pieces)


def fence(*groups):
    leaves, tree = jax.tree.flatten(groups)
    return jax.tree.unflatten(tree, lax.optimization_barrier(tuple(leaves)))


def split_kernel(info, tokens, to_core, to_z):
    core, z = info[0], info[4]
    for q in range(4):
        to_core[q] = tokens[2 * q + 1 - core]
        to_z[q] = tokens[4 * (1 - z) + q]


def pack_kernel(right, info, tokens, received, *outs):
    core, z, x, y = info[0], info[4], info[5], info[6]
    mine, here = (core, y) if right else (z, x)
    for k in range(4):
        place = lax.rem(here + k, 4)
        outs[k][mine] = tokens[2 * place + core if right else 4 * z + place]
        outs[k][1 - mine] = received[place]


def assemble_kernel(info, *refs):
    along_y, along_x, (right, left) = refs[:4], refs[4:8], refs[8:]
    x, y = info[5], info[6]
    for k in range(4):
        place_y = lax.rem(y + 4 - k, 4)
        place_x = lax.rem(x + 4 - k, 4)
        for h in range(2):
            right[2 * place_y + h] = along_y[k][h]
            left[4 * h + place_x] = along_x[k][h]


def local(kernel, name, outs, *args):
    return pl.pallas_call(
        kernel,
        grid_spec=pltpu.PrefetchScalarGridSpec(
            num_scalar_prefetch=1,
            grid=(),
            in_specs=[VMEM] * (len(args) - 1),
            out_specs=[VMEM] * len(outs),
        ),
        out_shape=[sds((n, LEN, BLK), BF16) for n in outs],
        compiler_params=PARAMS,
        name=name,
    )(*args)


def shifts(arrays, axis):
    return [lax.ppermute(a, axis, ring(4, k)) for k, a in enumerate(arrays, 1)]


def pack(right, info, tokens, received):
    kernel = functools.partial(pack_kernel, right)
    return local(kernel, "pack", [2] * 4, info, tokens, received)


def first_move(info, tokens):
    to_core, to_z = local(split_kernel, "split", [4, 4], info, tokens)
    own, *leaving = pack(True, info, tokens, swap(to_core))
    return [own, *shifts(leaving, "y"), flip(to_z)]


def second_move(info, tokens, along_y, from_z):
    own, *leaving = pack(False, info, tokens, from_z)
    return [*along_y, own, *shifts(leaving, "x")]


def assemble(info, *pieces):
    return local(assemble_kernel, "assemble", [8, 8], info, *pieces)


def swap(a):
    return lax.ppermute(a, "core", ring(2, 1))


def gather_left(left):
    return lax.all_gather(left, ("y", "core"), axis=0)


def from_next(a):
    return lax.ppermute(a, "x", ring(4, -1))


def from_prev(a):
    return lax.ppermute(a, "x", ring(4, 1))


def flip(a):
    return lax.ppermute(a, "z", ring(2, 1))


def gather_first(own):
    return [flip(own), from_next(own), from_prev(own)]


def gather_second(across, nxt, prv):
    return [from_next(nxt), flip(nxt), from_prev(across)]


def gather_third(far, across_nxt, across_prv):
    return [from_next(across_nxt[:3]), from_prev(across_prv[3:6]), flip(far[6:])]


def per_device(section_inputs, norm_gain, down_proj, up_proj, top_grad, lengths):
    core = lax.axis_index("core")
    stage = lax.axis_index("pipe")
    here_z = lax.axis_index("z")
    here_x = lax.axis_index("x")
    x = section_inputs[0]
    down_t = down_proj[0].T
    start = (1 - core) * LEN
    w = [up_proj[0], down_t, norm_gain]
    received = [
        swap(part)
        for part in (
            lax.dynamic_slice(x, (start, 0), (LEN, HALF)),
            lax.dynamic_slice(top_grad, (start, 0), (LEN, HALF)),
            *w,
        )
    ]
    length = lax.dynamic_slice(lengths, (0, core), (1, 1))[0, 0]
    info = jnp.stack(
        [core, length, stage, jnp.zeros_like(stage), here_z, here_x, lax.axis_index("y")]
    ).astype(jnp.int32)
    x_blocks, top, normed, w_blocks = prepare(info, x, top_grad, *w, *received)
    places = jnp.stack(
        [
            z * 4 + (here_x + dx) % 4
            for z, dx in (
                (here_z, 0),
                (1 - here_z, 0),
                (here_z, 1),
                (here_z, 3),
                (here_z, 2),
                (1 - here_z, 1),
                (1 - here_z, 3),
                (1 - here_z, 2),
            )
        ]
    ).astype(jnp.int32)

    def step(slot, received, before):
        return layer(slot, info, top, x_blocks, w_blocks, received, before)

    *state, leaving = step(0, None, ())
    above = move_down(0, leaving)
    moved = first_move(info, normed)
    above, moved, state, normed = fence(above, moved, state, normed)

    *state, leaving = step(1, above, state)
    above = move_down(1, leaving)
    moved_again = second_move(info, normed, moved[:4], moved[4])
    above, moved_again, state, normed = fence(above, moved_again, state, normed)

    *state, leaving = step(2, above, state)
    above = move_down(2, leaving)
    own_in, left_in = assemble(info, *moved_again)
    left_in = gather_left(left_in)
    nxt, prv = from_next(own_in), from_prev(own_in)
    above, nxt, prv, own_in, state = fence(above, nxt, prv, own_in, state)

    *state, leaving = step(3, above, state)
    above = move_down(3, leaving)
    far = [from_next(nxt[:4]), from_prev(prv[4:])]
    across = flip(own_in)
    above, far, across, state, own_in, prv = fence(above, far, across, state, own_in, prv)
    current, result, _ = step(4, above, state)

    moved = first_move(info, current)
    across_nxt = from_next(across)
    moved, across_nxt, prv, current, result = fence(moved, across_nxt, prv, current, result)

    moved_again = second_move(info, current, moved[:4], moved[4])
    across_prv = flip(prv)
    moved_again, across_prv, result = fence(moved_again, across_prv, result)

    own_out, left_out = assemble(info, *moved_again)
    left_out = gather_left(left_out)
    first_out = gather_first(own_out)
    halves = result.reshape(2, LOCAL, LEN, BLK)
    mine = lax.dynamic_index_in_dim(halves, core, 0, keepdims=False)
    other = swap(lax.dynamic_index_in_dim(halves, 1 - core, 0, keepdims=False))
    pair = jnp.where(core == 0, jnp.stack([mine, other]), jnp.stack([other, mine]))
    grads = pair.transpose(0, 2, 1, 3).reshape(1, 2 * LEN, HALF)
    rights_in = [[own_in], [across], [nxt], [prv], far, [across_nxt], [across_prv]]
    begun_in = factor(1.0, places, left_in, rights_in)
    first_out, begun_in, grads = fence(first_out, begun_in, grads)
    second_out = gather_second(*first_out)
    third_in = [from_next(across_nxt[:4]), from_prev(across_prv[4:])]
    last_in = lax.dynamic_index_in_dim(left_in, places[7], 1, keepdims=False)
    begun = factor(1.0, places, left_out, [[a] for a in (own_out, *first_out)])
    last_out = lax.dynamic_index_in_dim(left_out, places[7], 1, keepdims=False)
    second_out, third_in, begun, last_in, last_out = fence(
        second_out, third_in, begun, last_in, last_out
    )
    third_out = gather_third(*second_out)
    fac_in = finish(1.0 / TOKENS, begun_in, last_in, third_in)
    begun = factor(1.0, places, left_out, [[a] for a in second_out], begun, 4)
    third_out, begun, fac_in = fence(third_out, begun, fac_in)
    fac_out = finish(adapter_scale * adapter_scale / TOKENS, begun, last_out, third_out)
    return (grads, fac_in[None, None, None], fac_out[None, None, None])


def solution(mesh):
    fine = Mesh(mesh.devices.reshape(4, 2, 4, 4, 2), ("pipe", "z", "x", "y", "core"))
    dp = ("z", "x", "y")
    placed = (
        P("pipe", dp, "core"),
        P("pipe", "core"),
        P("pipe", "core", None),
        P("pipe", None, "core"),
        P(dp, "core"),
        P(dp, None),
    )
    return jax.shard_map(
        per_device,
        mesh=fine,
        in_specs=placed,
        out_specs=(
            P("pipe", dp, "core"),
            P("pipe", dp, "core", None, None),
            P("pipe", dp, "core", None, None),
        ),
        check_vma=False,
    )
```

```python
import functools

import jax
import jax.numpy as jnp
from jax import lax
from jax.experimental import pallas as pl
from jax.experimental.pallas import tpu as pltpu
from jax.sharding import Mesh, PartitionSpec as P

D = 6144
HALF = D // 2
R = 16
LEN = 64
TOKENS = 4096
BLK = 768
NBLK = D // BLK
LOCAL = HALF // BLK
STAGES = 4
CHUNKS = 2
ROWS = LEN // CHUNKS

adapter_scale = 0.5
epsilon_norm = 1e-05

F32 = jnp.float32
BF16 = jnp.bfloat16
VMEM = pl.BlockSpec(memory_space=pltpu.VMEM)
PARAMS = pltpu.CompilerParams(vmem_limit_bytes=12 * 2**20)


def sds(shape, dtype):
    return jax.ShapeDtypeStruct(shape, dtype)


def ring(size, by):
    return [(i, (i + by) % size) for i in range(size)]


def prepare_kernel(info, x, top, *refs):
    halves = (refs[:3], refs[5:8])
    others = refs[3:5]
    x_out, top_out, normed_out, w_out = refs[8:]
    core, length = info[0], info[1]
    valid = (lax.broadcasted_iota(jnp.int32, (LEN, 1), 0) < length).astype(F32)
    rows = pl.ds(pl.multiple_of(core * LEN, LEN), LEN)
    squares = jnp.zeros((LEN, 1), F32)
    for i in range(LOCAL):
        cols = slice(i * BLK, (i + 1) * BLK)
        for side, x_part, top_part, (up, down, gain) in (
            (core, x[rows, cols], top[rows, cols], halves[0]),
            (1 - core, others[0][:, cols], others[1][:, cols], halves[1]),
        ):
            place = side * LOCAL + i
            x_out[place] = x_part
            top_out[place] = (top_part.astype(F32) * valid).astype(BF16)
            w_out[place, 0:R] = up[:, cols]
            w_out[place, R : 2 * R] = down[:, cols]
            w_out[place, 2 * R :] = jnp.broadcast_to(gain[:, cols], (R, BLK))
            wide = x_part.astype(F32)
            squares += jnp.sum(wide * wide, axis=1, keepdims=True)
    inverse = 1.0 / jnp.sqrt(squares / D + epsilon_norm)
    for j in range(NBLK):
        gain = w_out[j, 2 * R : 2 * R + 1].astype(F32)
        normed_out[j] = (x_out[j].astype(F32) * inverse * gain * valid).astype(BF16)


def prepare(info, *args):
    blocks = sds((NBLK, LEN, BLK), BF16)
    return pl.pallas_call(
        prepare_kernel,
        grid_spec=pltpu.PrefetchScalarGridSpec(
            num_scalar_prefetch=1, grid=(), in_specs=[VMEM] * 10, out_specs=[VMEM] * 4
        ),
        out_shape=[blocks, blocks, blocks, sds((NBLK, 3 * R, BLK), BF16)],
        compiler_params=PARAMS,
        name="prepare",
    )(info, *args)


def layer_kernel(slot, info, top, x, w, *refs):
    received = refs[0] if slot else None
    current, result, leaving = refs[-3:]
    stage = info[2]
    chunk = slot - (STAGES - 1) + stage

    @pl.when(jnp.logical_and(chunk >= 0, chunk < CHUNKS))
    def _():
        rows = pl.ds(pl.multiple_of(chunk * ROWS, ROWS), ROWS)
        total = jnp.zeros((ROWS, R), F32)
        squares = jnp.zeros((ROWS, 1), F32)
        for j in range(NBLK):
            grad = top[j, rows]
            if slot:
                grad = jnp.where(stage == STAGES - 1, grad, received[j])
            current[j, rows] = grad
            total += lax.dot_general(
                grad, w[j, 0:R], (((1,), (1,)), ((), ())), preferred_element_type=F32
            )
            wide = x[j, rows].astype(F32)
            squares += jnp.sum(wide * wide, axis=1, keepdims=True)
        low = (adapter_scale * total).astype(BF16)
        inverse = 1.0 / jnp.sqrt(squares / D + epsilon_norm)
        inner = jnp.zeros((ROWS, 1), F32)

        def weighted(j):
            gain = w[j, 2 * R : 2 * R + 1].astype(F32)
            return gain * jnp.dot(low, w[j, R : 2 * R], preferred_element_type=F32)

        for j in range(NBLK):
            inner += jnp.sum(weighted(j) * x[j, rows].astype(F32), axis=1, keepdims=True)
        cube = inverse * inverse * inverse
        scale = cube * inner / D
        for j in range(NBLK):
            value = (
                current[j, rows].astype(F32)
                + inverse * weighted(j)
                - x[j, rows].astype(F32) * scale
            ).astype(BF16)
            result[j, rows] = value
            leaving[j] = value


def layer(slot, info, top, x, w, received, before):
    blocks = sds((NBLK, LEN, BLK), BF16)
    args = [top, x, w] + ([received] if slot else []) + list(before)
    at = len(args) - 1
    return pl.pallas_call(
        functools.partial(layer_kernel, slot),
        grid_spec=pltpu.PrefetchScalarGridSpec(
            num_scalar_prefetch=1, grid=(), in_specs=[VMEM] * len(args), out_specs=[VMEM] * 3
        ),
        out_shape=[blocks, blocks, sds((NBLK, ROWS, BLK), BF16)],
        input_output_aliases={at: 0, at + 1: 1} if before else {},
        compiler_params=PARAMS,
        name="layer",
    )(info, *args)


def move_down(slot, leaving):
    pairs = [(s, s - 1) for s in range(1, STAGES) if 0 <= slot - (STAGES - 1) + s < CHUNKS]
    return lax.ppermute(leaving, "pipe", pairs)


def factor_kernel(scale, counts, first, places, left, *refs):
    pieces, refs = refs[: sum(counts)], refs[sum(counts) :]
    before = refs[0] if first else None
    out, rows, cols, sems = refs[-4:]
    copies = []
    for n, count in enumerate(counts):
        chunk, pieces = pieces[:count], pieces[count:]
        pairs = [(left.at[:, places[first + n]], rows.at[n])]
        at = 0
        for piece in chunk:
            size = piece.shape[0]
            pairs.append((piece, cols.at[n, at : at + size]))
            at += size
        copies.append(
            [
                pltpu.make_async_copy(source, target, sems.at[n, i])
                for i, (source, target) in enumerate(pairs)
            ]
        )
        for copy in copies[n]:
            copy.start()
    for n in range(len(counts)):
        for copy in copies[n]:
            copy.wait()
        part = lax.dot_general(
            rows[n].reshape(8 * LEN, BLK),
            cols[n].reshape(8 * LEN, BLK),
            (((0,), (0,)), ((), ())),
            preferred_element_type=F32,
        )
        if n or first:
            part = (out if n else before)[...] + part
        out[...] = part * scale if scale != 1.0 and n == len(counts) - 1 else part


def factor(scale, places, left, rights, before=None, first=0):
    pieces = [piece for chunk in rights for piece in chunk]
    counts = tuple(len(chunk) for chunk in rights)
    begun = [] if before is None else [before]
    chunks = pltpu.VMEM((len(counts), 8, LEN, BLK), BF16)
    return pl.pallas_call(
        functools.partial(factor_kernel, scale, counts, first),
        grid_spec=pltpu.PrefetchScalarGridSpec(
            num_scalar_prefetch=1,
            grid=(),
            in_specs=[pl.BlockSpec(memory_space=pl.ANY)] * (1 + len(pieces))
            + [VMEM] * len(begun),
            out_specs=VMEM,
            scratch_shapes=[
                chunks,
                chunks,
                pltpu.SemaphoreType.DMA((len(counts), 1 + max(counts))),
            ],
        ),
        out_shape=sds((BLK, BLK), F32),
        compiler_params=pltpu.CompilerParams(vmem_limit_bytes=56 * 2**20),
        cost_estimate=pl.CostEstimate(
            flops=16 * LEN * BLK * BLK * len(counts),
            bytes_accessed=32 * LEN * BLK * len(counts) + 4 * BLK * BLK,
            transcendentals=0,
        ),
        name="factor",
    )(places, left, *pieces, *begun)


def finish_kernel(scale, begun, left, *refs):
    pieces, out = refs[:-1], refs[-1]
    cols = jnp.concatenate([piece[...].reshape(-1, BLK) for piece in pieces], axis=0)
    part = lax.dot_general(
        left[...].reshape(8 * LEN, BLK),
        cols,
        (((0,), (0,)), ((), ())),
        preferred_element_type=F32,
    )
    out[...] = (begun[...] + part) * scale


def finish(scale, begun, left, pieces):
    return pl.pallas_call(
        functools.partial(finish_kernel, scale),
        in_specs=[VMEM] * (2 + len(pieces)),
        out_specs=VMEM,
        out_shape=sds((BLK, BLK), F32),
        compiler_params=PARAMS,
        name="finish",
    )(begun, left, *pieces)


def fence(*groups):
    leaves, tree = jax.tree.flatten(groups)
    return jax.tree.unflatten(tree, lax.optimization_barrier(tuple(leaves)))


def split_kernel(info, tokens, to_core, to_z):
    core, z = info[0], info[4]
    for q in range(4):
        to_core[q] = tokens[2 * q + 1 - core]
        to_z[q] = tokens[4 * (1 - z) + q]


def pack_kernel(right, info, tokens, received, *outs):
    core, z, x, y = info[0], info[4], info[5], info[6]
    mine, here = (core, y) if right else (z, x)
    for k in range(4):
        place = lax.rem(here + k, 4)
        outs[k][mine] = tokens[2 * place + core if right else 4 * z + place]
        outs[k][1 - mine] = received[place]


def assemble_kernel(info, *refs):
    along_y, along_x, (right, left) = refs[:4], refs[4:8], refs[8:]
    x, y = info[5], info[6]
    for k in range(4):
        place_y = lax.rem(y + 4 - k, 4)
        place_x = lax.rem(x + 4 - k, 4)
        for h in range(2):
            right[2 * place_y + h] = along_y[k][h]
            left[4 * h + place_x] = along_x[k][h]


def local(kernel, name, outs, *args):
    return pl.pallas_call(
        kernel,
        grid_spec=pltpu.PrefetchScalarGridSpec(
            num_scalar_prefetch=1,
            grid=(),
            in_specs=[VMEM] * (len(args) - 1),
            out_specs=[VMEM] * len(outs),
        ),
        out_shape=[sds((n, LEN, BLK), BF16) for n in outs],
        compiler_params=PARAMS,
        name=name,
    )(*args)


def shifts(arrays, axis):
    return [lax.ppermute(a, axis, ring(4, k)) for k, a in enumerate(arrays, 1)]


def pack(right, info, tokens, received):
    kernel = functools.partial(pack_kernel, right)
    return local(kernel, "pack", [2] * 4, info, tokens, received)


def first_move(info, tokens):
    to_core, to_z = local(split_kernel, "split", [4, 4], info, tokens)
    own, *leaving = pack(True, info, tokens, swap(to_core))
    return [own, *shifts(leaving, "y"), flip(to_z)]


def second_move(info, tokens, along_y, from_z):
    own, *leaving = pack(False, info, tokens, from_z)
    return [*along_y, own, *shifts(leaving, "x")]


def assemble(info, *pieces):
    return local(assemble_kernel, "assemble", [8, 8], info, *pieces)


def swap(a):
    return lax.ppermute(a, "core", ring(2, 1))


def gather_left(left):
    return lax.all_gather(left, ("y", "core"), axis=0)


def from_next(a):
    return lax.ppermute(a, "x", ring(4, -1))


def from_prev(a):
    return lax.ppermute(a, "x", ring(4, 1))


def flip(a):
    return lax.ppermute(a, "z", ring(2, 1))


def gather_first(own):
    return [flip(own), from_next(own), from_prev(own)]


def gather_second(across, nxt, prv):
    return [from_next(nxt), flip(nxt), from_prev(across)]


def gather_third(far, across_nxt, across_prv):
    return [from_next(across_nxt[:3]), from_prev(across_prv[3:6]), flip(far[6:])]


def per_device(section_inputs, norm_gain, down_proj, up_proj, top_grad, lengths):
    core = lax.axis_index("core")
    stage = lax.axis_index("pipe")
    here_z = lax.axis_index("z")
    here_x = lax.axis_index("x")
    x = section_inputs[0]
    down_t = down_proj[0].T
    start = (1 - core) * LEN
    w = [up_proj[0], down_t, norm_gain]
    received = [
        swap(part)
        for part in (
            lax.dynamic_slice(x, (start, 0), (LEN, HALF)),
            lax.dynamic_slice(top_grad, (start, 0), (LEN, HALF)),
            *w,
        )
    ]
    length = lax.dynamic_slice(lengths, (0, core), (1, 1))[0, 0]
    info = jnp.stack(
        [core, length, stage, jnp.zeros_like(stage), here_z, here_x, lax.axis_index("y")]
    ).astype(jnp.int32)
    x_blocks, top, normed, w_blocks = prepare(info, x, top_grad, *w, *received)
    places = jnp.stack(
        [
            z * 4 + (here_x + dx) % 4
            for z, dx in (
                (here_z, 0),
                (1 - here_z, 0),
                (here_z, 1),
                (here_z, 3),
                (here_z, 2),
                (1 - here_z, 1),
                (1 - here_z, 3),
                (1 - here_z, 2),
            )
        ]
    ).astype(jnp.int32)

    def step(slot, received, before):
        return layer(slot, info, top, x_blocks, w_blocks, received, before)

    *state, leaving = step(0, None, ())
    above = move_down(0, leaving)
    moved = first_move(info, normed)
    above, moved, state, normed = fence(above, moved, state, normed)

    *state, leaving = step(1, above, state)
    above = move_down(1, leaving)
    moved_again = second_move(info, normed, moved[:4], moved[4])
    above, moved_again, state, normed = fence(above, moved_again, state, normed)

    *state, leaving = step(2, above, state)
    above = move_down(2, leaving)
    own_in, left_in = assemble(info, *moved_again)
    left_in = gather_left(left_in)
    nxt, prv = from_next(own_in), from_prev(own_in)
    above, nxt, prv, own_in, state = fence(above, nxt, prv, own_in, state)

    *state, leaving = step(3, above, state)
    above = move_down(3, leaving)
    far = [from_next(nxt[:4]), from_prev(prv[4:])]
    across = flip(own_in)
    above, far, across, state, own_in, prv = fence(above, far, across, state, own_in, prv)
    current, result, _ = step(4, above, state)

    moved = first_move(info, current)
    across_nxt = from_next(across)
    moved, across_nxt, prv, current, result = fence(moved, across_nxt, prv, current, result)

    moved_again = second_move(info, current, moved[:4], moved[4])
    across_prv = flip(prv)
    halves = result.reshape(2, LOCAL, LEN, BLK)
    mine = lax.dynamic_index_in_dim(halves, core, 0, keepdims=False)
    other = swap(lax.dynamic_index_in_dim(halves, 1 - core, 0, keepdims=False))
    moved_again, across_prv, mine, other, half_nxt = fence(
        moved_again, across_prv, mine, other, across_nxt[:4]
    )

    own_out, left_out = assemble(info, *moved_again)
    left_out = gather_left(left_out)
    first_out = gather_first(own_out)
    third_in = [from_next(half_nxt), from_prev(across_prv[4:])]
    pair = jnp.where(core == 0, jnp.stack([mine, other]), jnp.stack([other, mine]))
    grads = pair.transpose(0, 2, 1, 3).reshape(1, 2 * LEN, HALF)
    rights_in = [[own_in], [across], [nxt], [prv], far, [across_nxt], [across_prv]]
    begun_in = factor(1.0, places, left_in, rights_in)
    last_in = lax.dynamic_index_in_dim(left_in, places[7], 1, keepdims=False)
    first_out, third_in, begun_in, last_in, grads = fence(
        first_out, third_in, begun_in, last_in, grads
    )
    second_out = gather_second(*first_out)
    fac_in = finish(1.0 / TOKENS, begun_in, last_in, third_in)
    begun = factor(1.0, places, left_out, [[a] for a in (own_out, *first_out)])
    last_out = lax.dynamic_index_in_dim(left_out, places[7], 1, keepdims=False)
    second_out, begun, last_out, fac_in = fence(second_out, begun, last_out, fac_in)
    third_out = gather_third(*second_out)
    begun = factor(1.0, places, left_out, [[a] for a in second_out], begun, 4)
    third_out, begun = fence(third_out, begun)
    fac_out = finish(adapter_scale * adapter_scale / TOKENS, begun, last_out, third_out)
    return (grads, fac_in[None, None, None], fac_out[None, None, None])


def solution(mesh):
    fine = Mesh(mesh.devices.reshape(4, 2, 4, 4, 2), ("pipe", "z", "x", "y", "core"))
    dp = ("z", "x", "y")
    placed = (
        P("pipe", dp, "core"),
        P("pipe", "core"),
        P("pipe", "core", None),
        P("pipe", None, "core"),
        P(dp, "core"),
        P(dp, None),
    )
    return jax.shard_map(
        per_device,
        mesh=fine,
        in_specs=placed,
        out_specs=(
            P("pipe", dp, "core"),
            P("pipe", dp, "core", None, None),
            P("pipe", dp, "core", None, None),
        ),
        check_vma=False,
    )
```
